32 devices in a mesh: seq: 16 (over z, y, x), head: 2 (over core).
Axes of the slice: x: 2, y: 2, z: 4, core: 2. Of those that a mesh axis runs over, the one named last changes fastest.
Arguments:
- block_input: bfloat16 [4096, 1024], P('seq'), may hold values from -6 to 6
- value_first: bfloat16 [4096, 1024], P('seq', 'head'), may hold values from -6 to 6
- out_cotangent: bfloat16 [4096, 1024], P('seq'), may hold values from -6 to 6
- seq_lengths: int32 [2], replicated, may hold values from 1 to 40, 64 in all
- w_rkv: bfloat16 [3, 1024, 1024], P(None, 'seq', 'head'), may hold values from -0.1875 to 0.1875
- w_out: bfloat16 [1024, 1024], P('head', 'seq'), may hold values from -0.375 to 0.375
- ffn_key: bfloat16 [4096, 1024], P('head', 'seq'), may hold values from -0.1875 to 0.1875
- ffn_value: bfloat16 [4096, 1024], P('head', 'seq'), may hold values from -0.09375 to 0.09375
- channel_params: bfloat16 [19, 1024], P(None, 'seq'), may hold values from -7 to 2, as said below
- low_rank: bfloat16 [576, 1024], P(None, 'seq'), may hold values from -1.1 to 1.1, as said below
Outputs:
- block_output: bfloat16 [4096, 1024], P('seq')
- input_grad: float32 [4096, 1024], P('seq')
- value_first_grad: float32 [4096, 1024], P('seq', 'head')
- w_rkv_grad: float32 [3, 1024, 1024], P(None, 'seq', 'head')
- w_out_grad: float32 [1024, 1024], P('head', 'seq')
- ffn_key_grad: float32 [4096, 1024], P('head', 'seq')
- ffn_value_grad: float32 [4096, 1024], P('head', 'seq')
- channel_params_grad: float32 [19, 1024], P(None, ('seq', 'head'))
- low_rank_grad: float32 [576, 1024], P(None, ('seq', 'head'))
The draws below stay inside these ranges and needn't reach their ends.
Inputs may be any that keep to these rules, and one draw needn't show every extreme that they name: `seq_lengths`: 2 sequence lengths counted in blocks of 64 tokens, summing to 64; the longest has 40 blocks. `channel_params`: rows 0 to 3: layer norms' gains and biases; 4 to 10: token-shift coefficients; 11: decay bias; 12: rate bias; 13: value-first bias; 14: key normalization scale; 15: key rate scale; 16: bonus scale; 17, 18: group norm gain and bias. `low_rank`: rows 0 to 287 map features to the decay, rate, value-first and gate ranks in that order; the next 288 rows map those ranks back to features.
All inputs are finite; a program needn't handle non-finite values.
Results may differ from the reference program's by a relative error of at most 0.017.
Values may be sent and summed in bfloat16 or wider, within the bound.
A program may use at most 320 MiB of HBM per device.

```python
import math
from functools import partial
import jax
import jax.numpy as jnp
import numpy as np
from jax import lax

D = 1024
HEADS = 16
HEAD_SIZE = 64
FF = 4096
DECAY_RANK = 64
RATE_RANK = 64
VALUE_RANK = 32
GATE_RANK = 128
RANKS = 288
SPAN = 64
TOKENS = 4096
SPANS = 64
LONGEST = 40
SEQS = 2


def draw_channel_params(key, part):
    low_ends = jnp.array([0.6, -0.5, 0.6, -0.5, 0.0, 0.0, 0.0, 0.0, 0.0, 0.0, 0.0, -7.0, -4.0, -2.0, 0.5, 0.0, -1.0, 0.6, -0.5], jnp.float32)
    high_ends = jnp.array([1.4, 0.5, 1.4, 0.5, 1.0, 1.0, 1.0, 1.0, 1.0, 1.0, 1.0, -1.0, 0.5, 2.0, 1.5, 1.0, 1.0, 1.4, 0.5], jnp.float32)
    fraction = jax.random.uniform(key, (19, D), dtype=jnp.float32)
    return (low_ends[:, None] + (high_ends - low_ends)[:, None] * fraction).astype(jnp.bfloat16)


def draw_low_rank(key, part):
    row_ids = jnp.arange(2 * RANKS)
    first_end = RANKS + DECAY_RANK
    second_end = first_end + RATE_RANK
    third_end = second_end + VALUE_RANK
    scale_rows = jnp.where(row_ids < RANKS, D ** (-0.5), jnp.where(row_ids < first_end, DECAY_RANK ** (-0.5), jnp.where(row_ids < second_end, RATE_RANK ** (-0.5), jnp.where(row_ids < third_end, VALUE_RANK ** (-0.5), GATE_RANK ** (-0.5)))))
    noise_draw = jax.random.truncated_normal(key, -3.0, 3.0, (2 * RANKS, D), dtype=jnp.float32)
    return (noise_draw * scale_rows.astype(jnp.float32)[:, None]).astype(jnp.bfloat16)


def steps_of(key, shape, cuts, least, top_value):
    def one(axis_at, parts):
        draws = jax.random.uniform(jax.random.fold_in(jax.random.fold_in(key, 6), axis_at), (parts,), jnp.float32, least / len(cuts), top_value / len(cuts))
        return jnp.repeat(jnp.exp(draws), shape[axis_at] // parts).reshape((-1,) + (1,) * (len(shape) - axis_at - 1))

    level = one(*cuts[0])
    for cut in cuts[1:]:
        level = level * one(*cut)
    return level


def length_profile(count, total, bound, slope):
    loads = [(1 << 20) // math.isqrt(grade ** slope) + 1 for grade in range(2, count + 1)]
    rest, counts = total - bound - (count - 1), [1] * (count - 1)
    while rest > 0:
        movable = [i for i in range(count - 1) if counts[i] < bound]
        whole, remaining = sum([loads[i] for i in movable]), rest
        for i in movable:
            extra = min(bound - counts[i], max(1, remaining * loads[i] // whole), rest)
            counts[i] = counts[i] + extra
            rest = rest - extra
    return np.array([bound] + counts)


def ragged(key, amount, total, most, lean):
    if amount == 2:
        one = jax.random.randint(key, (), max(1, total - most), min(most, total - 1) + 1)
        return jnp.stack([one, total - one])
    tallies = jnp.asarray(length_profile(amount, total, most, lean), jnp.int32)
    couples = (amount - 1) // 2
    donor, receiver = tallies[1:1 + 2 * couples:2], tallies[2:2 + 2 * couples:2]
    room = jnp.minimum(donor - 1, most - receiver)
    shifted = jax.random.randint(jax.random.fold_in(key, 1), (couples,), 0, 1 << 20) % (room + 1)
    tallies = tallies.at[1:1 + 2 * couples:2].set(donor - shifted).at[2:2 + 2 * couples:2].set(receiver + shifted)
    return tallies[jax.random.permutation(jax.random.fold_in(key, 2), amount)]


def scatter_about(rng, shape, deviation, reach, cuts=(), held_as=jnp.bfloat16):
    values = jax.random.normal(rng, shape, jnp.float32) * deviation
    if len(cuts) > 0:
        values = steps_of(rng, shape, cuts, -0.22, 0.18) * values
    return jnp.clip(values, min=-reach, max=reach).astype(held_as)


def setup_inputs(seed: int = 0) -> dict:
    key_of = jax.random.split(jax.random.key(seed), 11)
    return {
        "block_input": scatter_about(key_of[0], (TOKENS, D), 1.0, 6.0, ((0, 16),)),
        "value_first": scatter_about(key_of[1], (TOKENS, D), 1.0, 6.0, ((0, 16), (1, 2))),
        "out_cotangent": scatter_about(key_of[2], (TOKENS, D), 1.0, 6.0, ((0, 16),)),
        "seq_lengths": ragged(key_of[3], SEQS, SPANS, LONGEST, 1).astype(jnp.int32),
        "w_rkv": scatter_about(key_of[4], (3, D, D), D ** -0.5, 0.1875, ((1, 16), (2, 2))),
        "w_out": scatter_about(key_of[5], (D, D), (D // 4) ** -0.5, 0.375, ((0, 2), (1, 16))),
        "ffn_key": scatter_about(key_of[6], (FF, D), D ** -0.5, 0.1875, ((0, 2), (1, 16))),
        "ffn_value": scatter_about(key_of[7], (FF, D), FF ** -0.5, 0.09375, ((0, 2), (1, 16))),
        "channel_params": draw_channel_params(jax.random.fold_in(key_of[10], 71), 0),
        "low_rank": draw_low_rank(jax.random.fold_in(key_of[10], 71), 0),
    }


norm_eps = 1e-05
group_eps = 0.00064
key_eps = 1e-06
highest = lax.Precision.HIGHEST

def dot_plain(left, right):
    return jnp.dot(left, right, preferred_element_type=jnp.float32)

def dot_rows(left, right):
    return lax.dot_general(left, right, (((1,), (1,)), ((), ())), preferred_element_type=jnp.float32)

def dot_tokens(left, right):
    return lax.dot_general(left, right, (((0,), (0,)), ((), ())), preferred_element_type=jnp.float32)

def dot_high(left, right):
    return jnp.dot(left, right, precision=highest, preferred_element_type=jnp.float32)

def tokens_high(left, right):
    return lax.dot_general(left, right, (((0,), (0,)), ((), ())), precision=highest, preferred_element_type=jnp.float32)

def layer_norm(inputs, gain, bias):
    centre = inputs - lax.optimization_barrier(jnp.mean(inputs, axis=-1, keepdims=True))
    spread = lax.optimization_barrier(jnp.mean(centre * centre, axis=-1, keepdims=True))
    return centre * lax.rsqrt(spread + norm_eps) * gain + bias

def divide_into_attention_parts(member, channels_per_attention_part):
    return member.reshape(member.shape[0], member.shape[1] // channels_per_attention_part, channels_per_attention_part)

def prepare(lookup_vector_mapped, payload_vector_mapped, first_layer_values_vector, forgetting_preactivation, learning_speed_preactivation, interpolation_preactivation, lookup_multiplier_vector, lookup_learning_coefficient, channels_per_attention_part):
    decay_rate = jnp.exp(-jnp.exp(-jax.nn.softplus(-forgetting_preactivation) - 0.5))
    in_rate = jax.nn.sigmoid(learning_speed_preactivation)
    payload_vector_combined = payload_vector_mapped + (first_layer_values_vector - payload_vector_mapped) * jax.nn.sigmoid(interpolation_preactivation)
    key_unit = divide_into_attention_parts(lookup_vector_mapped * lookup_multiplier_vector, channels_per_attention_part)
    key_unit = key_unit * lax.rsqrt(lax.optimization_barrier(jnp.sum(key_unit * key_unit, axis=-1, keepdims=True)) + key_eps)
    key_unit = key_unit.reshape(lookup_vector_mapped.shape)
    key_taken = key_unit * in_rate
    lookup_vector_modified = lookup_vector_mapped * (1.0 + (in_rate - 1.0) * lookup_learning_coefficient)
    return (decay_rate, key_unit, key_taken, payload_vector_combined, lookup_vector_modified)

def state_step(state_now, items):
    query_vector_lines, decay_rate, key_unit, key_taken, payload_vector_combined, lookup_vector_modified, reset_now = items
    state_now = state_now * (1.0 - reset_now)
    along_key = jnp.einsum('hij,hj->hi', state_now, key_unit, precision=highest)
    state_now = state_now * decay_rate[:, None, :] - along_key[:, :, None] * key_taken[:, None, :] + payload_vector_combined[:, :, None] * lookup_vector_modified[:, None, :]
    return (state_now, jnp.einsum('hij,hj->hi', state_now, query_vector_lines, precision=highest))

def previous_position_interpolation(sequence_restart_markers, memory_matrix_before, query_vector_lines, lookup_vector_mapped, payload_vector_mapped, first_layer_values_vector, forgetting_preactivation, learning_speed_preactivation, interpolation_preactivation, emission_sigmoid_multiplier, lookup_multiplier_vector, lookup_learning_coefficient, extra_diagonal_coefficient, channel_gain_after_standardize, channel_offset_after_standardize):
    channels_per_attention_part = memory_matrix_before.shape[-1]
    decay_rate, key_unit, key_taken, payload_vector_combined, lookup_vector_modified = prepare(lookup_vector_mapped, payload_vector_mapped, first_layer_values_vector, forgetting_preactivation, learning_speed_preactivation, interpolation_preactivation, lookup_multiplier_vector, lookup_learning_coefficient, channels_per_attention_part)
    items = tuple((divide_into_attention_parts(member, channels_per_attention_part) for member in (query_vector_lines, decay_rate, key_unit, key_taken, payload_vector_combined, lookup_vector_modified))) + (sequence_restart_markers,)
    state_out, read_out = lax.scan(jax.checkpoint(state_step), memory_matrix_before, items)
    centre = read_out - lax.optimization_barrier(jnp.mean(read_out, axis=-1, keepdims=True))
    spread = lax.optimization_barrier(jnp.mean(centre * centre, axis=-1, keepdims=True))
    standardized_layer_entry = centre * lax.rsqrt(spread + group_eps) * divide_into_attention_parts(channel_gain_after_standardize[None, :], channels_per_attention_part) + divide_into_attention_parts(channel_offset_after_standardize[None, :], channels_per_attention_part)
    extra_diagonal_contribution = lax.optimization_barrier(jnp.sum(divide_into_attention_parts(query_vector_lines * lookup_vector_modified * extra_diagonal_coefficient, channels_per_attention_part), axis=-1, keepdims=True)) * divide_into_attention_parts(payload_vector_combined, channels_per_attention_part)
    attention_branch_outcome = (standardized_layer_entry + extra_diagonal_contribution).reshape(query_vector_lines.shape) * emission_sigmoid_multiplier
    return (attention_branch_outcome, state_out)

def project(mixed_rows, rkv_cols, maps_in, maps_out, chan_params):
    first_end = DECAY_RANK
    second_end = first_end + RATE_RANK
    third_end = second_end + VALUE_RANK
    query_vector_lines = dot_plain(mixed_rows[0], rkv_cols[0])
    lookup_vector_mapped = dot_plain(mixed_rows[2], rkv_cols[1])
    payload_vector_mapped = dot_plain(mixed_rows[3], rkv_cols[2])
    decay_hidden = jnp.tanh(dot_rows(mixed_rows[1], maps_in[:first_end]))
    decay_low = decay_hidden.astype(jnp.bfloat16)
    forgetting_preactivation = chan_params[11] + dot_plain(decay_low, maps_out[:first_end])
    rate_low = dot_rows(mixed_rows[4], maps_in[first_end:second_end]).astype(jnp.bfloat16)
    learning_speed_preactivation = chan_params[12] + dot_plain(rate_low, maps_out[first_end:second_end])
    mix_low = dot_rows(mixed_rows[3], maps_in[second_end:third_end]).astype(jnp.bfloat16)
    interpolation_preactivation = chan_params[13] + dot_plain(mix_low, maps_out[second_end:third_end])
    gate_hidden = jax.nn.sigmoid(dot_rows(mixed_rows[5], maps_in[third_end:]))
    gate_low = gate_hidden.astype(jnp.bfloat16)
    emission_sigmoid_multiplier = dot_plain(gate_low, maps_out[third_end:])
    saved = (decay_hidden, decay_low, rate_low, mix_low, gate_hidden, gate_low)
    return (saved, (query_vector_lines, lookup_vector_mapped, payload_vector_mapped, forgetting_preactivation, learning_speed_preactivation, interpolation_preactivation, emission_sigmoid_multiplier))

def project_back(mixed_rows, rkv_cols, maps_in, maps_out, saved, grads_in):
    first_end = DECAY_RANK
    second_end = first_end + RATE_RANK
    third_end = second_end + VALUE_RANK
    decay_hidden, decay_low, rate_low, mix_low, gate_hidden, gate_low = saved
    d_recept, d_key, d_value, d_decay, d_rate, d_mix, d_gate = grads_in
    recept_low = d_recept.astype(jnp.bfloat16)
    key_low = d_key.astype(jnp.bfloat16)
    value_low = d_value.astype(jnp.bfloat16)
    rkv_grad = jnp.stack([dot_tokens(mixed_rows[0], recept_low), dot_tokens(mixed_rows[2], key_low), dot_tokens(mixed_rows[3], value_low)])
    maps_float = maps_in.astype(jnp.float32)
    decay_back = d_decay.astype(jnp.bfloat16)
    decay_rank = dot_rows(decay_back, maps_out[:first_end]) * (1.0 - decay_hidden * decay_hidden)
    rate_back = d_rate.astype(jnp.bfloat16)
    rate_rank = dot_rows(rate_back, maps_out[first_end:second_end])
    mix_back_low = d_mix.astype(jnp.bfloat16)
    mix_rank = dot_rows(mix_back_low, maps_out[second_end:third_end])
    gate_back = d_gate.astype(jnp.bfloat16)
    gate_rank = dot_rows(gate_back, maps_out[third_end:]) * gate_hidden * (1.0 - gate_hidden)
    out_grads = jnp.concatenate([dot_tokens(decay_low, decay_back), dot_tokens(rate_low, rate_back), dot_tokens(mix_low, mix_back_low), dot_tokens(gate_low, gate_back)], axis=0)
    in_grads = jnp.concatenate([tokens_high(decay_rank, mixed_rows[1].astype(jnp.float32)), tokens_high(rate_rank, mixed_rows[4].astype(jnp.float32)), tokens_high(mix_rank, mixed_rows[3].astype(jnp.float32)), tokens_high(gate_rank, mixed_rows[5].astype(jnp.float32))], axis=0)
    grad_recept = dot_rows(recept_low, rkv_cols[0])
    grad_decay = dot_high(decay_rank, maps_float[:first_end])
    grad_key = dot_rows(key_low, rkv_cols[1])
    grad_value = dot_rows(value_low, rkv_cols[2]) + dot_high(mix_rank, maps_float[second_end:third_end])
    grad_rate = dot_high(rate_rank, maps_float[first_end:second_end])
    grad_gate = dot_high(gate_rank, maps_float[third_end:])
    bias_grads = jnp.stack([lax.optimization_barrier(jnp.sum(d_decay, axis=0)), lax.optimization_barrier(jnp.sum(d_rate, axis=0)), lax.optimization_barrier(jnp.sum(d_mix, axis=0))])
    return ([grad_recept, grad_decay, grad_key, grad_value, grad_rate, grad_gate], rkv_grad, in_grads, out_grads, bias_grads)

def shift_diff(standardized_layer_entry, edge_row, keep_mask):
    previous = jnp.concatenate([edge_row, standardized_layer_entry[:-1]], axis=0) * keep_mask
    return previous - standardized_layer_entry

def mix_back(grads_list, coeffs, shifted_diff, keep_mask):
    direct = jnp.zeros_like(shifted_diff)
    carried = jnp.zeros_like(shifted_diff)
    for column, grad_rows in enumerate(grads_list):
        direct = direct + grad_rows * (1.0 - coeffs[column])
        carried = carried + grad_rows * coeffs[column]
    coeff_grads = jnp.stack([lax.optimization_barrier(jnp.sum(grad_rows * shifted_diff, axis=0)) for grad_rows in grads_list])
    return (direct, carried * keep_mask, coeff_grads)

def reference(block_input, value_first, out_cotangent, seq_lengths, w_rkv, w_out, ffn_key, ffn_value, channel_params, low_rank):
    params = channel_params.astype(jnp.float32)
    position = jnp.arange(TOKENS, dtype=jnp.int32)
    starts = ((jnp.cumsum(seq_lengths) - seq_lengths) * SPAN).astype(jnp.int32)
    sequence_restart_markers = jnp.any(position[:, None] == starts[None, :], axis=1).astype(jnp.float32)
    keep_mask = (1.0 - sequence_restart_markers)[:, None]
    inputs_float = block_input.astype(jnp.float32)
    no_edge = jnp.zeros((1, D), jnp.float32)
    normed_one = layer_norm(inputs_float, params[0], params[1])
    diff_one = shift_diff(normed_one, no_edge, keep_mask)
    mixed_rows = [(normed_one + diff_one * params[4 + column]).astype(jnp.bfloat16) for column in range(6)]
    maps_in = low_rank[:RANKS]
    maps_out = low_rank[RANKS:]
    saved, mixer_args = project(mixed_rows, w_rkv, maps_in, maps_out, params)
    query_vector_lines, lookup_vector_mapped, payload_vector_mapped, forgetting_preactivation, learning_speed_preactivation, interpolation_preactivation, emission_sigmoid_multiplier = mixer_args
    first_layer_values_vector = value_first.astype(jnp.float32)
    fixed_params = tuple((params[row_index] for row_index in range(14, 19)))
    block_len = math.gcd(TOKENS, 1024)
    block_count = TOKENS // block_len

    def split(member):
        return member.reshape((block_count, block_len) + member.shape[1:])
    token_items = (query_vector_lines, lookup_vector_mapped, payload_vector_mapped, first_layer_values_vector, forgetting_preactivation, learning_speed_preactivation, interpolation_preactivation, emission_sigmoid_multiplier)
    state_zero = jnp.zeros((HEADS, HEAD_SIZE, HEAD_SIZE), jnp.float32)

    def forward_block(state_now, items):
        attention_branch_outcome, state_out = previous_position_interpolation(items[0], state_now, *items[1:], *fixed_params)
        return (state_out, (attention_branch_outcome, state_now))
    _, (mixed_blocks, state_blocks) = lax.scan(forward_block, state_zero, (split(sequence_restart_markers),) + tuple((split(member) for member in token_items)))
    mixer_low = mixed_blocks.reshape(TOKENS, D).astype(jnp.bfloat16)
    residual_one = inputs_float + dot_plain(mixer_low, w_out)
    normed_two = layer_norm(residual_one, params[2], params[3])
    diff_two = shift_diff(normed_two, no_edge, keep_mask)
    mixed_ffn = (normed_two + diff_two * params[10]).astype(jnp.bfloat16)
    hidden_pre = dot_rows(mixed_ffn, ffn_key)
    hidden_low = jnp.square(jax.nn.relu(hidden_pre)).astype(jnp.bfloat16)
    block_output = (residual_one + dot_plain(hidden_low, ffn_value)).astype(jnp.bfloat16)
    cot_float = out_cotangent.astype(jnp.float32)
    value_grad = dot_tokens(hidden_low, out_cotangent)
    hidden_grad = dot_rows(out_cotangent, ffn_value)
    pre_low = (hidden_grad * 2.0 * jax.nn.relu(hidden_pre)).astype(jnp.bfloat16)
    key_grad = dot_tokens(pre_low, mixed_ffn)
    ffn_in_grad = dot_plain(pre_low, ffn_key)
    direct_two, carried_two, coeff_two = mix_back([ffn_in_grad], params[10:11], diff_two, keep_mask)
    normed_two_grad = direct_two + jnp.concatenate([carried_two[1:], no_edge], axis=0)
    _, norm_two_back = jax.vjp(layer_norm, residual_one, params[2], params[3])
    resid_part, gain_two, bias_two = norm_two_back(normed_two_grad)
    residual_grad = cot_float + resid_part
    attend_low = residual_grad.astype(jnp.bfloat16)
    out_grad = dot_tokens(mixer_low, attend_low)
    mixer_grad = dot_rows(attend_low, w_out)

    def backward_block(state_grad, items):
        reset_block, state_now, grad_block = (items[0], items[1], items[2])
        primal_args = (state_now,) + tuple(items[3:]) + fixed_params
        _, mixer_back = jax.vjp(partial(previous_position_interpolation, reset_block), *primal_args)
        grads_all = mixer_back((grad_block, state_grad))
        return (grads_all[0], (grads_all[1:9], grads_all[9:]))
    _, (token_grads, param_grads) = lax.scan(backward_block, state_zero, (split(sequence_restart_markers), state_blocks, split(mixer_grad)) + tuple((split(member) for member in token_items)), reverse=True)
    token_grads = tuple((member.reshape(TOKENS, D) for member in token_grads))
    param_grads = [lax.optimization_barrier(jnp.sum(member, axis=0)) for member in param_grads]
    d_recept, d_key, d_value, d_first, d_decay, d_rate, d_mix, d_gate = token_grads
    mixed_grads, rkv_grad, in_grads, out_grads, bias_grads = project_back(mixed_rows, w_rkv, maps_in, maps_out, saved, (d_recept, d_key, d_value, d_decay, d_rate, d_mix, d_gate))
    direct_one, carried_one, coeff_one = mix_back(mixed_grads, params[4:10], diff_one, keep_mask)
    normed_one_grad = direct_one + jnp.concatenate([carried_one[1:], no_edge], axis=0)
    _, norm_one_back = jax.vjp(layer_norm, inputs_float, params[0], params[1])
    input_part, gain_one, bias_one = norm_one_back(normed_one_grad)
    input_grad = residual_grad + input_part
    channel_grad = jnp.concatenate([jnp.stack([gain_one, bias_one, gain_two, bias_two]), coeff_one, coeff_two, bias_grads, jnp.stack(param_grads)], axis=0)
    low_rank_grad = jnp.concatenate([in_grads, out_grads], axis=0)
    return (block_output, input_grad, d_first, rkv_grad, out_grad, key_grad, value_grad, channel_grad, low_rank_grad)
```

```python
from functools import partial

import jax
import jax.numpy as jnp
from jax import lax
from jax.experimental import pallas as pl
from jax.experimental.pallas import tpu as pltpu
from jax.sharding import PartitionSpec as P

HEAD_SIZE = 64
DECAY_RANK = 64
RATE_RANK = 64
VALUE_RANK = 32
RANKS = 288
SPAN = 64


norm_eps = 1e-05
group_eps = 0.00064
key_eps = 1e-06
highest = lax.Precision.HIGHEST


def shifted(array, axis, by):
    size = lax.axis_size(axis)
    pairs = [(i, i + by) for i in range(size) if 0 <= i + by < size]
    return lax.ppermute(array, axis, pairs)


def dot_plain(left, right):
    return jnp.dot(left, right, preferred_element_type=jnp.float32)


def dot_rows(left, right):
    return lax.dot_general(
        left, right, (((1,), (1,)), ((), ())), preferred_element_type=jnp.float32
    )


def dot_tokens(left, right):
    return lax.dot_general(
        left, right, (((0,), (0,)), ((), ())), preferred_element_type=jnp.float32
    )


def dot_high(left, right):
    return jnp.dot(left, right, precision=highest, preferred_element_type=jnp.float32)


def tokens_high(left, right):
    return lax.dot_general(
        left, right, (((0,), (0,)), ((), ())), precision=highest, preferred_element_type=jnp.float32
    )


def layer_norm(inputs, gain, bias):
    centre = inputs - jnp.mean(inputs, axis=-1, keepdims=True)
    spread = jnp.mean(centre * centre, axis=-1, keepdims=True)
    return centre * lax.rsqrt(spread + norm_eps) * gain + bias


def raw_dot(left, right, kind):
    dims = {"nn": ((1,), (0,)), "nt": ((1,), (1,)), "tn": ((0,), (0,))}[kind]
    return lax.dot_general(
        left, right, (dims, ((), ())), precision=highest, preferred_element_type=jnp.float32
    )


@partial(jax.custom_vjp, nondiff_argnums=(2,))
def mul(left, right, kind):
    return raw_dot(left, right, kind)


def mul_fwd(left, right, kind):
    return raw_dot(left, right, kind), (left, right)


def mul_bwd(kind, saved, grad):
    left, right = saved
    if kind == "nn":
        return raw_dot(grad, right, "nt"), raw_dot(left, grad, "tn")
    if kind == "nt":
        return raw_dot(grad, right, "nn"), raw_dot(grad, left, "tn")
    return raw_dot(right, grad, "nt"), raw_dot(left, grad, "nn")


mul.defvjp(mul_fwd, mul_bwd)


@jax.custom_vjp
def solved(lower, right, inverse):
    return raw_dot(inverse, right, "nn")


def solved_fwd(lower, right, inverse):
    out = raw_dot(inverse, right, "nn")
    return out, (inverse, out)


def solved_bwd(saved, grad):
    inverse, out = saved
    right_grad = raw_dot(inverse, grad, "tn")
    return -raw_dot(right_grad, out, "nt"), right_grad, jnp.zeros_like(inverse)


solved.defvjp(solved_fwd, solved_bwd)


def grid_masks():
    row = lax.broadcasted_iota(jnp.int32, (SPAN, SPAN), 0)
    column = lax.broadcasted_iota(jnp.int32, (SPAN, SPAN), 1)
    return row, column


def inverse_of(lowers):
    row, column = grid_masks()
    eye = (row == column).astype(jnp.float32)
    outs = None
    size = 1
    while size < SPAN:
        shift = size.bit_length() - 1
        rb, cb = row >> shift, column >> shift
        mask = ((rb >> 1) == (cb >> 1)) & (rb > cb)
        parts = [jnp.where(mask, lower, 0.0) for lower in lowers]
        if outs is None:
            outs = [eye - part for part in parts]
        else:
            halves = [raw_dot(out, part, "nn") for out, part in zip(outs, parts)]
            outs = [out - raw_dot(half, out, "nn") for out, half in zip(outs, halves)]
        size *= 2
    return outs


def prepare(key_raw, value_raw, first, decay_pre, rate_pre, mix_pre, key_scale, rate_scale):
    log_decay = -jnp.exp(-jax.nn.softplus(-decay_pre) - 0.5)
    in_rate = jax.nn.sigmoid(rate_pre)
    value_new = value_raw + (first - value_raw) * jax.nn.sigmoid(mix_pre)
    scaled = key_raw * key_scale
    key_unit = scaled * lax.rsqrt(jnp.sum(scaled * scaled, axis=-1, keepdims=True) + key_eps)
    key_taken = key_unit * in_rate
    key_final = key_raw * (1.0 + (in_rate - 1.0) * rate_scale)
    return log_decay, key_unit, key_taken, value_new, key_final


@jax.custom_vjp
def quarters(whole):
    half = whole.shape[0] // 2
    return whole[:half, :half], whole[:half, half:], whole[half:, :half], whole[half:, half:]


def quarters_fwd(whole):
    return quarters(whole), None


def quarters_bwd(_, grads):
    upper = jnp.concatenate([grads[0], grads[1]], axis=1)
    lower = jnp.concatenate([grads[2], grads[3]], axis=1)
    return (jnp.concatenate([upper, lower], axis=0),)


quarters.defvjp(quarters_fwd, quarters_bwd)


def span_start(recept, log_decay, key_unit, key_taken, key_final):
    row, column = grid_masks()
    inclusive = (row >= column).astype(jnp.float32)
    log_total = mul(inclusive, log_decay, "nn")
    gamma = jnp.exp(log_total)
    before = jnp.exp(log_total - log_decay)
    inverse = jnp.exp(-log_total)
    unit_back = key_unit * before
    key_hat = key_final * inverse
    taken_hat = key_taken * inverse
    strict = (row > column).astype(jnp.float32)
    upper = jnp.concatenate([strict, strict], axis=1)
    under = jnp.concatenate([inclusive, inclusive], axis=1)
    asking = jnp.concatenate([unit_back, recept * gamma], axis=0)
    asked_of = jnp.concatenate([key_hat, taken_hat], axis=0)
    scores = mul(asking, asked_of, "nt") * jnp.concatenate([upper, under], axis=0)
    cross_key, lower, read_key, read_taken = quarters(scores)
    end = jnp.exp(jnp.sum(log_decay, axis=0, keepdims=True))
    return gamma, unit_back, key_hat, taken_hat, lower, cross_key, read_key, read_taken, end


def span_end(recept, value_new, start, inverse):
    gamma, unit_back, key_hat, taken_hat, lower, cross_key, read_key, read_taken, end = start
    row, column = grid_masks()
    carried = solved(lower, unit_back, inverse)
    base = solved(lower, mul(cross_key, value_new, "nn"), inverse)
    tilde = recept * gamma
    asked = tilde - mul(read_taken, carried, "nn")
    own = mul(read_key, value_new, "nn") - mul(read_taken, base, "nn")
    eye = (row == column).astype(jnp.float32)
    matrix = (eye - mul(carried, taken_hat, "tn")) * end
    offset_state = (mul(value_new, key_hat, "tn") - mul(base, taken_hat, "tn")) * end
    return asked, own, matrix, offset_state


def output_of(read, recept, key_final, value_new, gate, bonus, gain, bias):
    centre = read - jnp.mean(read, axis=-1, keepdims=True)
    spread = jnp.mean(centre * centre, axis=-1, keepdims=True)
    normed = centre * lax.rsqrt(spread + group_eps) * gain + bias
    extra = jnp.sum(recept * key_final * bonus, axis=-1, keepdims=True) * value_new
    return (normed + extra) * gate


def heads_of(ref):
    lanes = ref.shape[-1] // HEAD_SIZE
    whole = ref[...].astype(jnp.float32)
    return [whole[:, i * HEAD_SIZE : (i + 1) * HEAD_SIZE] for i in range(lanes)]


def parts_kernel(r, k, v, f, d, a, m, rows, inverse_out, maps_out, asked_out, own_out):
    tokens = list(zip(*[heads_of(x) for x in (r, k, v, f, d, a, m)]))
    params = heads_of(rows)
    ready = [prepare(*t[1:], p[0:1], p[1:2]) for t, p in zip(tokens, params)]
    starts = [span_start(t[0], x[0], x[1], x[2], x[4]) for t, x in zip(tokens, ready)]
    inverses = inverse_of([s[4] for s in starts])
    asks, owns = [], []
    for i, (t, x, s, inv) in enumerate(zip(tokens, ready, starts, inverses)):
        asked, own, matrix, offset_state = span_end(t[0], x[3], s, inv)
        inverse_out[0, i] = inv
        maps_out[0, i, 0:HEAD_SIZE, :] = matrix
        maps_out[0, i, HEAD_SIZE : 2 * HEAD_SIZE, :] = offset_state
        asks.append(asked)
        owns.append(own)
    asked_out[...] = jnp.concatenate(asks, axis=1)
    own_out[...] = jnp.concatenate(owns, axis=1)


def finish(recept, key_raw, value_raw, first, rate_pre, mix_pre, gate, p, read):
    zero = jnp.zeros_like(rate_pre)
    _, _, _, value_new, key_final = prepare(
        key_raw, value_raw, first, zero, rate_pre, mix_pre, p[0:1], p[1:2]
    )
    return output_of(read, recept, key_final, value_new, gate, p[2:3], p[3:4], p[4:5])


def output_kernel(r, k, v, f, a, m, g, rows, asked, own, state, out):
    outs = []
    tokens = zip(*[heads_of(x) for x in (r, k, v, f, a, m, g, rows, asked, own)])
    for i, t in enumerate(tokens):
        read = t[9] + raw_dot(t[8], state[0, i], "nt")
        outs.append(finish(*t[:8], read))
    out[...] = jnp.concatenate(outs, axis=1).astype(out.dtype)


def state_back_kernel(r, k, v, f, a, m, g, rows, asked, own, state, cot, state_grad):
    tokens = zip(*[heads_of(x) for x in (r, k, v, f, a, m, g, rows, asked, own, cot)])
    for i, t in enumerate(tokens):
        read = t[9] + raw_dot(t[8], state[0, i], "nt")
        _, back = jax.vjp(partial(finish, *t[:8]), read)
        state_grad[0, i] = raw_dot(back(t[10])[0], t[8], "tn")


def whole_span(inverse, state, recept, key_raw, value_raw, first, decay_pre, rate_pre, mix_pre, gate, *p):
    log_decay, key_unit, key_taken, value_new, key_final = prepare(
        key_raw, value_raw, first, decay_pre, rate_pre, mix_pre, p[0], p[1]
    )
    start = span_start(recept, log_decay, key_unit, key_taken, key_final)
    asked, own, matrix, offset_state = span_end(recept, value_new, start, inverse)
    read = own + mul(asked, state, "nt")
    out = output_of(read, recept, key_final, value_new, gate, p[2], p[3], p[4])
    return out, mul(state, matrix, "nn") + offset_state


def back_kernel(r, k, v, f, d, a, m, g, rows, inverse, state, cot, next_grad, *outs):
    tokens = zip(*[heads_of(x) for x in (r, k, v, f, d, a, m, g, rows, cot)])
    columns = []
    for i, t in enumerate(tokens):
        p = tuple(t[8][j : j + 1] for j in range(5))
        _, back = jax.vjp(partial(whole_span, inverse[0, i], state[0, i]), *t[:8], *p)
        columns.append(back((t[9], next_grad[0, i])))
    for j in range(8):
        outs[j][...] = jnp.concatenate([c[j] for c in columns], axis=1).astype(outs[j].dtype)
    for j in range(5):
        outs[8][0, j : j + 1, :] = jnp.concatenate([c[8 + j] for c in columns], axis=1)
    outs[8][0, 5:8, :] = jnp.zeros((3, outs[8].shape[2]), jnp.float32)


LANES = 128
PAIR = LANES // HEAD_SIZE
token_spec = pl.BlockSpec((SPAN, LANES), lambda z, h: (z, h))
rows_spec = pl.BlockSpec((8, LANES), lambda z, h: (0, h))
square_spec = pl.BlockSpec((1, PAIR, HEAD_SIZE, HEAD_SIZE), lambda z, h: (z, h, 0, 0))
maps_spec = pl.BlockSpec((1, PAIR, 2 * HEAD_SIZE, HEAD_SIZE), lambda z, h: (z, h, 0, 0))
sums_spec = pl.BlockSpec((1, 8, LANES), lambda z, h: (z, 0, h))


def run(kernel, arrays, in_specs, out_specs, out_shapes, flops):
    tokens, width = arrays[0].shape
    moved = sum(a.size * a.dtype.itemsize for a in arrays)
    return pl.pallas_call(
        kernel,
        grid=(tokens // SPAN, width // LANES),
        in_specs=in_specs,
        out_specs=out_specs,
        out_shape=out_shapes,
        compiler_params=pltpu.CompilerParams(vmem_limit_bytes=32 * 1024 * 1024),
        cost_estimate=pl.CostEstimate(flops=flops, bytes_accessed=2 * moved, transcendentals=0),
    )(*arrays)


def joined(earlier, later):
    size = later.shape[-1]
    return jnp.einsum("...ij,...jk->...ik", earlier, later[..., :size, :], precision=highest) + jnp.concatenate(
        [jnp.zeros_like(later[..., :size, :]), later[..., size:, :]], axis=-2
    )


def before(own, place):
    count = lax.axis_size("seq")
    size = own.shape[-1]
    eye = jnp.broadcast_to(jnp.eye(size, dtype=own.dtype), own[:, :size].shape)
    total, ahead = own, jnp.concatenate([eye, jnp.zeros_like(eye)], axis=1)
    step = 1
    while step < count:
        pairs = [(i, i ^ step) for i in range(count)]
        other = lax.ppermute(total.astype(jnp.bfloat16), "seq", pairs).astype(jnp.float32)
        upper = (place & step) != 0
        ahead = jnp.where(upper, joined(other, ahead), ahead)
        if 2 * step < count:
            total = joined(jnp.where(upper, other, total), jnp.where(upper, total, other))
        step *= 2
    return ahead[:, size:]


def head_sum(part):
    own = part.astype(jnp.bfloat16)
    pairs = [(i, i ^ 1) for i in range(lax.axis_size("head"))]
    other = lax.ppermute(own, "head", pairs)
    return own.astype(jnp.float32) + other.astype(jnp.float32)


def gathered(shard):
    return lax.all_gather(shard, "seq", axis=0, tiled=True)


def scattered(full):
    return lax.psum_scatter(
        full.astype(jnp.bfloat16), "seq", scatter_dimension=0, tiled=True
    ).astype(jnp.float32)

def project(mixed_rows, rkv_cols, maps_in, maps_out, chan_params):
    first_end = DECAY_RANK
    second_end = first_end + RATE_RANK
    third_end = second_end + VALUE_RANK
    query_vector_lines = dot_plain(mixed_rows[0], rkv_cols[0])
    lookup_vector_mapped = dot_plain(mixed_rows[2], rkv_cols[1])
    payload_vector_mapped = dot_plain(mixed_rows[3], rkv_cols[2])
    decay_hidden = jnp.tanh(dot_plain(mixed_rows[1], maps_in[:, :first_end]))
    decay_low = decay_hidden.astype(jnp.bfloat16)
    forgetting_preactivation = chan_params[11] + dot_rows(decay_low, maps_out[:, :first_end])
    rate_low = dot_plain(mixed_rows[4], maps_in[:, first_end:second_end]).astype(jnp.bfloat16)
    learning_speed_preactivation = chan_params[12] + dot_rows(
        rate_low, maps_out[:, first_end:second_end]
    )
    mix_low = dot_plain(mixed_rows[3], maps_in[:, second_end:third_end]).astype(jnp.bfloat16)
    interpolation_preactivation = chan_params[13] + dot_rows(
        mix_low, maps_out[:, second_end:third_end]
    )
    gate_hidden = jax.nn.sigmoid(dot_plain(mixed_rows[5], maps_in[:, third_end:]))
    gate_low = gate_hidden.astype(jnp.bfloat16)
    emission_sigmoid_multiplier = dot_rows(gate_low, maps_out[:, third_end:])
    saved = (decay_hidden, decay_low, rate_low, mix_low, gate_hidden, gate_low)
    return (
        saved,
        (
            query_vector_lines,
            lookup_vector_mapped,
            payload_vector_mapped,
            forgetting_preactivation,
            learning_speed_preactivation,
            interpolation_preactivation,
            emission_sigmoid_multiplier,
        ),
    )


def rank_dot(ranks, maps_in):
    high = ranks.astype(jnp.bfloat16)
    low = (ranks - high.astype(jnp.float32)).astype(jnp.bfloat16)
    return dot_rows(high, maps_in) + dot_rows(low, maps_in)


def rank_tokens(rows, ranks):
    high = ranks.astype(jnp.bfloat16)
    low = (ranks - high.astype(jnp.float32)).astype(jnp.bfloat16)
    return dot_tokens(rows, high) + dot_tokens(rows, low)


def project_back(mixed_rows, rkv_cols, maps_in, maps_out, saved, grads_in):
    first_end = DECAY_RANK
    second_end = first_end + RATE_RANK
    third_end = second_end + VALUE_RANK
    decay_hidden, decay_low, rate_low, mix_low, gate_hidden, gate_low = saved
    recept_low, key_low, value_low, decay_back, rate_back, mix_back_low, gate_back = grads_in
    rkv_grad = [
        dot_tokens(mixed_rows[0], recept_low),
        dot_tokens(mixed_rows[2], key_low),
        dot_tokens(mixed_rows[3], value_low),
    ]
    decay_rank = dot_plain(decay_back, maps_out[:, :first_end]) * (
        1.0 - decay_hidden * decay_hidden
    )
    rate_rank = dot_plain(rate_back, maps_out[:, first_end:second_end])
    mix_rank = dot_plain(mix_back_low, maps_out[:, second_end:third_end])
    gate_rank = dot_plain(gate_back, maps_out[:, third_end:]) * gate_hidden * (1.0 - gate_hidden)
    out_grads = jnp.concatenate(
        [
            dot_tokens(decay_back, decay_low),
            dot_tokens(rate_back, rate_low),
            dot_tokens(mix_back_low, mix_low),
            dot_tokens(gate_back, gate_low),
        ],
        axis=1,
    )
    in_grads = jnp.concatenate(
        [
            rank_tokens(mixed_rows[1], decay_rank),
            rank_tokens(mixed_rows[4], rate_rank),
            rank_tokens(mixed_rows[3], mix_rank),
            rank_tokens(mixed_rows[5], gate_rank),
        ],
        axis=1,
    )
    grad_recept = dot_rows(recept_low, rkv_cols[0])
    grad_decay = rank_dot(decay_rank, maps_in[:, :first_end])
    grad_key = dot_rows(key_low, rkv_cols[1])
    grad_value = dot_rows(value_low, rkv_cols[2]) + rank_dot(
        mix_rank, maps_in[:, second_end:third_end]
    )
    grad_rate = rank_dot(rate_rank, maps_in[:, first_end:second_end])
    grad_gate = rank_dot(gate_rank, maps_in[:, third_end:])
    return (
        [grad_recept, grad_decay, grad_key, grad_value, grad_rate, grad_gate],
        rkv_grad,
        in_grads,
        out_grads,
    )


def shift_diff(standardized_layer_entry, edge_row, keep_mask):
    previous = jnp.concatenate([edge_row, standardized_layer_entry[:-1]], axis=0) * keep_mask
    return previous - standardized_layer_entry


def mix_back(grads_list, coeffs, shifted_diff, keep_mask):
    direct = jnp.zeros_like(shifted_diff)
    carried = jnp.zeros_like(shifted_diff)
    for column, grad_rows in enumerate(grads_list):
        direct = direct + grad_rows * (1.0 - coeffs[column])
        carried = carried + grad_rows * coeffs[column]
    coeff_grads = jnp.stack([jnp.sum(grad_rows * shifted_diff, axis=0) for grad_rows in grads_list])
    return (direct, carried * keep_mask, coeff_grads)


def on_device(
    block_input,
    value_first,
    out_cotangent,
    seq_lengths,
    w_rkv,
    w_out,
    ffn_key,
    ffn_value,
    channel_params,
    low_rank,
):
    tokens_dev, width = block_input.shape
    local_width = w_rkv.shape[2]
    spans = tokens_dev // SPAN
    heads_dev = local_width // HEAD_SIZE
    place = lax.axis_index("seq")
    offset = lax.axis_index("head") * local_width
    small = jnp.concatenate([low_rank, channel_params], axis=0)
    small_rows = small.shape[0]
    packed = -(-small_rows // 128) * 128
    small_all = gathered(jnp.pad(small, ((0, packed - small_rows), (0, 0))).T)
    rkv_all = lax.all_gather(w_rkv, "seq", axis=1, tiled=True)
    out_all = gathered(w_out.T)
    key_all = gathered(ffn_key.T)
    value_all = gathered(ffn_value.T)
    params = small_all[:, 2 * RANKS : small_rows].astype(jnp.float32).T
    local_params = lax.dynamic_slice_in_dim(params, offset, local_width, 1)
    maps_in = small_all[:, :RANKS]
    maps_out = lax.dynamic_slice_in_dim(small_all[:, RANKS : 2 * RANKS], offset, local_width, 0)
    position = place * tokens_dev + jnp.arange(tokens_dev, dtype=jnp.int32)
    order = jnp.arange(seq_lengths.shape[0])
    earlier = jnp.where(order[None, :] < order[:, None], seq_lengths[None, :], 0)
    starts = jnp.sum(earlier, axis=1) * SPAN
    resets = jnp.any(position[:, None] == starts[None, :], axis=1).astype(jnp.float32)
    keep_mask = (1.0 - resets)[:, None]
    keep_span = (1.0 - resets.reshape(spans, SPAN)[:, 0])[:, None, None, None]
    inputs_float = block_input.astype(jnp.float32)
    normed_one = layer_norm(inputs_float, params[0], params[1])
    edge_one = shifted(normed_one[-1:], "seq", 1)
    diff_one = shift_diff(normed_one, edge_one, keep_mask)
    mixed_rows = [
        (normed_one + diff_one * params[4 + column]).astype(jnp.bfloat16) for column in range(6)
    ]
    saved, mixer_args = project(mixed_rows, rkv_all, maps_in, maps_out, local_params)
    recept, key_raw, value_raw, decay_pre, rate_pre, mix_pre, gate = mixer_args
    rows = jnp.pad(local_params[14:19], ((0, 3), (0, 0)))
    wide = jax.ShapeDtypeStruct((tokens_dev, local_width), jnp.float32)
    wide_low = jax.ShapeDtypeStruct((tokens_dev, local_width), jnp.bfloat16)
    square = jax.ShapeDtypeStruct((spans, heads_dev, HEAD_SIZE, HEAD_SIZE), jnp.float32)
    double = jax.ShapeDtypeStruct((spans, heads_dev, 2 * HEAD_SIZE, HEAD_SIZE), jnp.float32)
    sums = jax.ShapeDtypeStruct((spans, 8, local_width), jnp.float32)
    inverse, maps, asked, own = run(
        parts_kernel,
        (recept, key_raw, value_raw, value_first, decay_pre, rate_pre, mix_pre, rows),
        [token_spec] * 7 + [rows_spec],
        [square_spec, maps_spec, token_spec, token_spec],
        [square, double, wide, wide],
        2 * 10**9,
    )
    span_mats = maps[:, :, :HEAD_SIZE] * keep_span
    maps = jnp.concatenate([span_mats, maps[:, :, HEAD_SIZE:]], axis=2)
    upto = [maps[0]]
    for z in range(1, spans):
        upto.append(joined(upto[-1], maps[z]))
    state_first = before(upto[-1], place)
    states = jnp.stack(
        [state_first]
        + [
            jnp.einsum("hij,hjk->hik", state_first, m[:, :HEAD_SIZE], precision=highest)
            + m[:, HEAD_SIZE:]
            for m in upto[:-1]
        ]
    ) * keep_span
    mixer_low = run(
        output_kernel,
        (recept, key_raw, value_raw, value_first, rate_pre, mix_pre, gate, rows, asked, own, states),
        [token_spec] * 7 + [rows_spec] + [token_spec] * 2 + [square_spec],
        token_spec,
        wide_low,
        10**8,
    )
    residual_one = inputs_float + head_sum(dot_rows(mixer_low, out_all))
    normed_two = layer_norm(residual_one, params[2], params[3])
    edge_two = shifted(normed_two[-1:], "seq", 1)
    diff_two = shift_diff(normed_two, edge_two, keep_mask)
    mixed_ffn = (normed_two + diff_two * params[10]).astype(jnp.bfloat16)
    hidden_pre = dot_plain(mixed_ffn, key_all)
    hidden_low = jnp.square(jax.nn.relu(hidden_pre)).astype(jnp.bfloat16)
    ffn_out = head_sum(dot_rows(hidden_low, value_all))
    block_output = (residual_one + ffn_out).astype(jnp.bfloat16)
    cot_float = out_cotangent.astype(jnp.float32)
    value_shard = scattered(dot_tokens(out_cotangent, hidden_low))
    hidden_grad = dot_plain(out_cotangent, value_all)
    pre_low = (hidden_grad * 2.0 * jax.nn.relu(hidden_pre)).astype(jnp.bfloat16)
    key_shard = scattered(dot_tokens(mixed_ffn, pre_low))
    ffn_in_grad = dot_rows(pre_low, key_all)
    direct_two, carried_two, coeff_two = mix_back([ffn_in_grad], params[10:11], diff_two, keep_mask)
    from_next_two = shifted(carried_two[:1], "seq", -1)
    normed_two_grad = direct_two + jnp.concatenate([carried_two[1:], from_next_two], axis=0)
    _, norm_two_back = jax.vjp(layer_norm, residual_one, params[2], params[3])
    resid_part, gain_two, bias_two = norm_two_back(normed_two_grad)
    residual_grad = cot_float + head_sum(resid_part)
    attend_low = residual_grad.astype(jnp.bfloat16)
    out_shard = scattered(dot_tokens(attend_low, mixer_low))
    mixer_grad = dot_plain(attend_low, out_all)
    read_grads = run(
        state_back_kernel,
        (recept, key_raw, value_raw, value_first, rate_pre, mix_pre, gate, rows, asked, own, states, mixer_grad),
        [token_spec] * 7 + [rows_spec] + [token_spec] * 2 + [square_spec, token_spec],
        square_spec,
        square,
        10**8,
    ) * keep_span
    grads, tails = [None] * spans, [None] * spans
    grad_first = read_grads[spans - 1]
    tail = span_mats[spans - 1]
    tails[spans - 2] = tail
    grads[spans - 2] = grad_first
    for z in range(spans - 2, -1, -1):
        grad_first = read_grads[z] + jnp.einsum(
            "hij,hkj->hik", grad_first, span_mats[z], precision=highest
        )
        tail = jnp.einsum("hij,hjk->hik", span_mats[z], tail, precision=highest)
        if z > 0:
            grads[z - 1], tails[z - 1] = grad_first, tail
    count = lax.axis_size("seq")
    state_grad = before(
        jnp.concatenate([jnp.swapaxes(tail, 1, 2), grad_first], axis=1), count - 1 - place
    )
    next_grads = jnp.stack(
        [
            g + jnp.einsum("hij,hkj->hik", state_grad, t, precision=highest)
            for g, t in zip(grads[:-1], tails[:-1])
        ]
        + [state_grad]
    )
    next_grads, value_shard = lax.optimization_barrier((next_grads, value_shard))
    back = run(
        back_kernel,
        (recept, key_raw, value_raw, value_first, decay_pre, rate_pre, mix_pre, gate, rows, inverse, states, mixer_grad, next_grads),
        [token_spec] * 8 + [rows_spec] + [square_spec] * 2 + [token_spec, square_spec],
        [token_spec] * 8 + [sums_spec],
        [wide_low, wide_low, wide_low, wide, wide, wide, wide, wide_low, sums],
        4 * 10**9,
    )
    d_recept, d_key, d_value, d_first, d_decay, d_rate, d_mix, d_gate, param_sums = back
    bias_grads = jnp.stack(
        [jnp.sum(d_decay, axis=0), jnp.sum(d_rate, axis=0), jnp.sum(d_mix, axis=0)]
    )
    lows = [x.astype(jnp.bfloat16) for x in (d_recept, d_key, d_value, d_decay, d_rate, d_mix, d_gate)]
    mixed_grads, rkv_grad, in_grads, out_grads = project_back(
        mixed_rows, rkv_all, maps_in, maps_out, saved, lows
    )
    mixed_grads, rkv_grad, key_shard, out_shard = lax.optimization_barrier(
        (mixed_grads, rkv_grad, key_shard, out_shard)
    )
    direct_one, carried_one, coeff_one = mix_back(mixed_grads, params[4:10], diff_one, keep_mask)
    from_next_one = shifted(carried_one[:1], "seq", -1)
    normed_one_grad = direct_one + jnp.concatenate([carried_one[1:], from_next_one], axis=0)
    _, norm_one_back = jax.vjp(layer_norm, inputs_float, params[0], params[1])
    input_part, gain_one, bias_one = norm_one_back(normed_one_grad)
    input_grad = residual_grad + head_sum(input_part)
    full_rows = jnp.concatenate(
        [jnp.stack([gain_one, bias_one, gain_two, bias_two]), coeff_one, coeff_two], axis=0
    )
    head_rows = jnp.concatenate([bias_grads, jnp.sum(param_sums, axis=0)[:5]], axis=0)
    placed = lax.dynamic_update_slice_in_dim(
        jnp.zeros((width, out_grads.shape[1] + head_rows.shape[0]), jnp.float32),
        jnp.concatenate([out_grads, head_rows.T], axis=1),
        offset,
        0,
    )
    small_grad = jnp.concatenate([in_grads, placed, full_rows.T], axis=1)
    rkv_sum = scattered(jnp.concatenate(rkv_grad, axis=1))
    small_sum = scattered(
        jnp.pad(small_grad, ((0, 0), (0, packed - small_rows)))
    )
    low_shard, channel_shard = halves(small_sum, out_grads.shape[1], small_rows)
    return (
        block_output,
        input_grad,
        d_first,
        jnp.transpose(rkv_sum.reshape(-1, 3, local_width), (1, 0, 2)),
        out_shard.T,
        key_shard.T,
        value_shard.T,
        channel_shard,
        low_shard,
    )


def halves(part, ranks, used):
    total = lax.psum_scatter(part, "head", scatter_dimension=0, tiled=True).T
    low = total[: 2 * ranks]
    head_rows = total[2 * ranks : 2 * ranks + 8]
    full_rows = total[2 * ranks + 8 : used]
    return low, jnp.concatenate([full_rows, head_rows], axis=0)


def solution(mesh):
    return jax.shard_map(
        on_device,
        mesh=mesh,
        in_specs=(
            P("seq", None),
            P("seq", "head"),
            P("seq", None),
            P(),
            P(None, "seq", "head"),
            P("head", "seq"),
            P("head", "seq"),
            P("head", "seq"),
            P(None, "seq"),
            P(None, "seq"),
        ),
        out_specs=(
            P("seq", None),
            P("seq", None),
            P("seq", "head"),
            P(None, "seq", "head"),
            P("head", "seq"),
            P("head", "seq"),
            P("head", "seq"),
            P(None, ("seq", "head")),
            P(None, ("seq", "head")),
        ),
        check_vma=False,
    )
```
